256 devices in a mesh: section: 16 (over y_lo, z), ctx: 16 (over y_hi, x, core).
Axes of the slice: x: 4, y: 4 (y_hi: 2, y_lo: 2; y = y_hi * 2 + y_lo), z: 8, core: 2. Of those that a mesh axis runs over, the one named last changes fastest.
Arguments:
- projected_up: bfloat16 [16, 2048, 3, 6144], P('section', 'ctx'), may hold values from -12 to 12
- projected_down: bfloat16 [16, 2048, 3, 6144], P('section', 'ctx'), may hold values from -12 to 12
- lengths_up: int32 [16, 8], P('section'), may hold values from 16 to 1024, as said below
- lengths_down: int32 [16, 8], P('section'), may hold values from 16 to 1024, as said below
- pattern_up: int32 [16, 16, 16], P('section'), may hold values from 0 to 1, as said below
- pattern_down: int32 [16, 16, 16], P('section'), may hold values from 0 to 1, as said below
Outputs:
- attended_up: bfloat16 [16, 2048, 6144], P('section', 'ctx')
- attended_down: bfloat16 [16, 2048, 6144], P('section', 'ctx')
The draws below stay inside these ranges and needn't reach their ends.
Inputs may be any that keep to these rules, and one draw needn't show every extreme that they name: `lengths_up`: each section's 8 lengths are multiples of 16 and sum to 2048; the last one is 16, and exactly one of them is 1024. `lengths_down`: each section's 8 lengths are multiples of 16 and sum to 2048; the last one is 16, and exactly one of them is 1024. `pattern_up`: entries are 0 or 1 and the diagonal is 1. `pattern_down`: entries are 0 or 1 and the diagonal is 1.
All inputs are finite; a program needn't handle non-finite values.
Results may differ from the reference program's by a relative error of at most 0.0033.
Values may be sent and summed in bfloat16 or wider, within the bound.
No kernel may reach another device: no remote copies, remote signals or barrier semaphores. Data moves between devices by JAX's collectives and lax.ppermute only.
A program may use at most 128 MiB of HBM per device.

```python
import math
import jax
import jax.numpy as jnp
from jax import lax

HEAD_DIM = 128
BLOCK = 128
UNIT = 16
SEGS = 8
D = 6144
SECTIONS = 16
TOKENS = 2048
NB = 16


def section_lengths(key):
    cut_key, place_key = jax.random.split(key)
    remaining = TOKENS // (2 * UNIT) - 1
    shuffled = jax.random.permutation(cut_key, remaining - 1) + 1
    cut_points = jnp.sort(shuffled[:SEGS - 3]).astype(jnp.int32)
    bounds = jnp.concatenate([jnp.zeros((1,), jnp.int32), cut_points, jnp.array([remaining], jnp.int32)])
    smaller = ((bounds[1:] - bounds[:-1]) * UNIT).astype(jnp.int32)
    place = jax.random.randint(place_key, (), 0, SEGS - 1)
    index = jnp.arange(SEGS - 1, dtype=jnp.int32)
    before = smaller[jnp.minimum(index, SEGS - 3)]
    after = smaller[jnp.maximum(index - 1, 0)]
    largest = jnp.full((SEGS - 1,), TOKENS // 2, jnp.int32)
    leading = jnp.where(index < place, before, jnp.where(index == place, largest, after))
    return jnp.concatenate([leading, jnp.array([UNIT], jnp.int32)]).astype(jnp.int32)


def block_pattern(key):
    first_key, second_key = jax.random.split(key)
    density = jax.random.randint(first_key, (), 15, 90)
    random_levels = jax.random.randint(second_key, (NB, NB), 0, 100)
    diagonal = jnp.arange(NB)[:, None] == jnp.arange(NB)[None, :]
    return ((random_levels < density) | diagonal).astype(jnp.int32)


def projections(key, key_scale):
    base_key = jax.random.fold_in(key, 0)
    shape = (SECTIONS, TOKENS, 3, D)
    spread = jnp.array([1.0, key_scale, 1.0], jnp.float32).reshape(1, 1, 3, 1)
    values = jax.random.truncated_normal(base_key, -4.0, 4.0, shape, jnp.float32) * spread
    return values.astype(jnp.bfloat16)


def draw_projected_up(key, part):
    key = jax.random.fold_in(key, 31)
    return projections(key, 2.0)


def draw_projected_down(key, part):
    key = jax.random.fold_in(key, 37)
    return projections(key, 2.0)


def draw_lengths_up(key, part):
    key = jax.random.fold_in(key, 11)
    return jax.vmap(section_lengths)(jax.random.split(key, SECTIONS))


def draw_lengths_down(key, part):
    key = jax.random.fold_in(key, 13)
    return jax.vmap(section_lengths)(jax.random.split(key, SECTIONS))


def draw_pattern_up(key, part):
    key = jax.random.fold_in(key, 17)
    return jax.vmap(block_pattern)(jax.random.split(key, SECTIONS))


def draw_pattern_down(key, part):
    key = jax.random.fold_in(key, 19)
    return jax.vmap(block_pattern)(jax.random.split(key, SECTIONS))


def setup_inputs(seed: int = 0) -> dict:
    splits = jax.random.split(jax.random.key(seed), 7)
    projected_up = draw_projected_up(jax.random.fold_in(splits[6], 71), 0)
    projected_down = draw_projected_down(jax.random.fold_in(splits[6], 71), 0)
    lengths_up = draw_lengths_up(jax.random.fold_in(splits[6], 71), 0)
    lengths_down = draw_lengths_down(jax.random.fold_in(splits[6], 71), 0)
    pattern_up = draw_pattern_up(jax.random.fold_in(splits[6], 71), 0)
    pattern_down = draw_pattern_down(jax.random.fold_in(splits[6], 71), 0)
    return {"projected_up": projected_up, "projected_down": projected_down, "lengths_up": lengths_up, "lengths_down": lengths_down, "pattern_up": pattern_up, "pattern_down": pattern_down}


masked_score = -1e+30

def segment_labels(lengths, token_count):
    bounds = jnp.cumsum(lengths)
    positions = jnp.arange(token_count, dtype=jnp.int32)
    return lax.optimization_barrier(jnp.sum((positions[:, None] >= bounds[None, :]).astype(jnp.int32), axis=1))

def allowed_mask(lengths, pattern):
    token_count = pattern.shape[0] * BLOCK
    labels = segment_labels(lengths, token_count)
    widened = jnp.repeat(jnp.repeat(pattern, BLOCK, axis=0), BLOCK, axis=1)
    return (widened == 1) & (labels[:, None] == labels[None, :])

def head_attention(operands, allowed):
    queries, key_rows, value_rows = operands
    scores = lax.dot_general(queries, key_rows, (((1,), (1,)), ((), ())), preferred_element_type=jnp.float32)
    scores = scores * (1.0 / math.sqrt(HEAD_DIM))
    scores = jnp.where(allowed, scores, masked_score)
    largest = lax.optimization_barrier(jnp.max(scores, axis=1, keepdims=True))
    exponentials = jnp.exp(scores - largest)
    totals = lax.optimization_barrier(jnp.sum(exponentials, axis=1, keepdims=True))
    weights = exponentials.astype(jnp.bfloat16)
    combined = jnp.dot(weights, value_rows, preferred_element_type=jnp.float32)
    return (combined / totals).astype(jnp.bfloat16)

def attend(projected, lengths, pattern):
    token_count = projected.shape[0]
    allowed = allowed_mask(lengths, pattern)
    per_head = projected.reshape(token_count, 3, -1, HEAD_DIM).transpose(1, 2, 0, 3)
    result = lax.map(lambda operands: head_attention(operands, allowed), (per_head[0], per_head[1], per_head[2]))
    return result.transpose(1, 0, 2).reshape(token_count, -1)

def reference(projected_up, projected_down, lengths_up, lengths_down, pattern_up, pattern_down):
    section_count = projected_up.shape[0]

    def from_below(section):
        source = jnp.mod(section + section_count - 1, section_count).astype(jnp.int32)
        return attend(projected_up[source], lengths_up[source], pattern_up[source])

    def from_above(section):
        source = jnp.mod(section + 1, section_count).astype(jnp.int32)
        return attend(projected_down[source], lengths_down[source], pattern_down[source])
    sections = jnp.arange(section_count, dtype=jnp.int32)
    return (lax.map(from_below, sections), lax.map(from_above, sections))
```

```python
import functools
import math

import jax
import jax.numpy as jnp
from jax import lax
from jax.experimental import pallas as pl
from jax.experimental.pallas import tpu as pltpu
from jax.sharding import PartitionSpec as P

HEAD_DIM = 128
BLOCK = 128
TALL = 2
WIDE = 4
GROUP = 3
CHIPS = 4
CUT_VMEM = 60 * 1024 * 1024

masked_score = -1e30
exponent_scale = math.log2(math.e) / math.sqrt(HEAD_DIM)

IN_HBM = pl.BlockSpec(memory_space=pl.ANY)
IN_SMEM = pl.BlockSpec(memory_space=pltpu.SMEM)


def carry(sources, targets, held, arrived, left):
    arrivals, departures = [], []
    for slot, (source, target) in enumerate(zip(sources, targets)):
        arrivals.append(pltpu.make_async_copy(source, held.at[slot], arrived.at[slot]))
        departures.append(pltpu.make_async_copy(held.at[slot], target, left.at[slot]))
    for arrival in arrivals:
        arrival.start()
    for arrival, departure in zip(arrivals, departures):
        arrival.wait()
        departure.start()
    for departure in departures:
        departure.wait()


def carry_scratch(count, shape):
    return [
        pltpu.VMEM((count, *shape), jnp.bfloat16),
        pltpu.SemaphoreType.DMA((count,)),
        pltpu.SemaphoreType.DMA((count,)),
    ]


def columns_of(side, place, offset, width):
    chip = side * CHIPS + (place ^ offset)
    return pl.ds(pl.multiple_of(chip * width, width), width)


def copied(plan, inputs, shapes, position, name, piece=None):
    piece = piece or shapes[0][-3:]
    count = len(plan(None, [None] * len(inputs), [None] * len(shapes), True))

    def kernel(position, *refs):
        ins, outs = refs[: len(inputs)], refs[len(inputs) : len(inputs) + len(shapes)]
        pairs = plan(position, ins, outs, False)
        carry([pair[0] for pair in pairs], [pair[1] for pair in pairs], *refs[-3:])

    return pl.pallas_call(
        kernel,
        out_shape=[jax.ShapeDtypeStruct(shape, jnp.bfloat16) for shape in shapes],
        in_specs=[IN_SMEM] + [IN_HBM] * len(inputs),
        out_specs=[IN_HBM] * len(shapes),
        scratch_shapes=carry_scratch(count, piece),
        compiler_params=pltpu.CompilerParams(vmem_limit_bytes=CUT_VMEM),
        name=name,
    )(position, *inputs)


def cut_from(rows, position, side, offset, width):
    return rows.at[:, :, columns_of(position[0] ^ side, position[1], offset, width)]


def cut_side(rows, position, piece, side):
    def plan(position, ins, outs, dry):
        if dry:
            return range(CHIPS)
        return [
            (cut_from(ins[0], position, side, offset, piece[-1]), outs[0].at[offset])
            for offset in range(CHIPS)
        ]

    return copied(plan, [rows], [(CHIPS, *piece)], position, "cut_side")[0]


def cut_both(up, down, position, piece, offsets):
    def plan(position, ins, outs, dry):
        if dry:
            return range(2 * len(offsets))
        pairs = []
        for out, offset in zip(outs, offsets):
            for part in range(2):
                source = cut_from(ins[part], position, part, offset, piece[-1])
                pairs.append((source, out.at[part]))
        return pairs

    return copied(plan, [up, down], [(2, *piece)] * len(offsets), position, "cut_both")


def cut_each(rows, position, piece, side):
    def plan(position, ins, outs, dry):
        if dry:
            return range(CHIPS)
        return [
            (cut_from(ins[0], position, side, offset, piece[-1]), outs[offset])
            for offset in range(CHIPS)
        ]

    return copied(plan, [rows], [piece] * CHIPS, position, "cut_each")


def regroup(spread, position):
    piece = spread[0].shape[1:]

    def plan(position, ins, outs, dry):
        if dry:
            return range(2 * CHIPS)
        return [
            (ins[index].at[side], outs[side].at[index])
            for side in (1, 0)
            for index in range(CHIPS)
        ]

    return copied(plan, spread, [(CHIPS, *piece)] * 2, position, "regroup")


def separate(pieces, position):
    shape = pieces.shape[1:]

    def plan(position, ins, outs, dry):
        if dry:
            return range(CHIPS - 1)
        return [(ins[0].at[index + 1], outs[index]) for index in range(CHIPS - 1)]

    return copied(plan, [pieces], [shape] * (CHIPS - 1), position, "separate")


def gather(sources, position):
    arrays = [array for array, _ in sources]
    piece = (2, *arrays[0].shape[-2:])

    def plan(position, ins, outs, dry):
        if dry:
            return range(CHIPS)
        return [
            (part(ins[index], where).at[pl.ds(1, 2)], outs[0].at[index])
            for index, (_, where) in enumerate(sources)
        ]

    return copied(plan, arrays, [(CHIPS, *piece)], position, "gather")[0]


def part(ref, where):
    return ref if where is None else ref.at[where]


def join(pieces, position):
    tokens, width = pieces[0].shape
    count = len(pieces)

    def plan(position, ins, outs, dry):
        if dry:
            return range(count)
        if len(ins) == 1:
            return [
                (ins[0].at[chip], outs[0].at[:, pl.ds(chip * width, width)])
                for chip in range(count)
            ]
        pairs = []
        for index, ref in enumerate(ins):
            side, offset = index // CHIPS, index % CHIPS
            columns = columns_of(position[0] ^ side, position[1], offset, width)
            pairs.append((ref, outs[0].at[:, columns]))
        return pairs

    inputs = pieces if isinstance(pieces, list) else [pieces]
    shape = (tokens, count * width)
    return copied(plan, inputs, [shape], position, "join", (tokens, width))[0]


def attend_kernel(places, apart, lengths, pattern, position, *refs):
    pieces = refs[: 2 * CHIPS]
    near_other, far_other = refs[2 * CHIPS : 2 * CHIPS + 2]
    scratch = refs[-9:] if apart else refs[-8:]
    asked, held, scores, largest, totals, combined, listed, arrived = scratch[-8:]
    outs = refs[2 * CHIPS + 2 : -len(scratch)]
    out_ref = scratch[0] if apart else outs[0]
    blocks = held.shape[0]
    group_heads = largest.shape[0]
    tile = TALL * BLOCK
    core = position[2]

    def block_of(piece, core):
        return (position[0] ^ (piece // CHIPS)) * (2 * CHIPS) + (
            (position[1] ^ (piece % CHIPS)) * 2 + core
        )

    copies = []
    for piece in range(2 * CHIPS):
        chip = block_of(piece, core) // 2
        copies.append((part(pieces[piece], places[piece]).at[0], asked.at[chip]))
        mine = part(pieces[piece], places[piece]).at[pl.ds(1, 2)]
        copies.append((mine, held.at[block_of(piece, core)]))
        other = (near_other if piece < CHIPS else far_other).at[piece % CHIPS]
        if other.shape[0] == 3:
            other = other.at[pl.ds(1, 2)]
        copies.append((other, held.at[block_of(piece, 1 - core)]))
    copies = [
        pltpu.make_async_copy(source, target, arrived.at[index])
        for index, (source, target) in enumerate(copies)
    ]
    for copy in copies:
        copy.start()

    bounds = []
    bound = jnp.int32(0)
    for clip in range(lengths.shape[0]):
        bound = bound + lengths[clip]
        bounds.append(bound)

    def labels(tokens):
        found = jnp.zeros(tokens.shape, jnp.int32)
        for bound in bounds:
            found = found + (tokens >= bound).astype(jnp.int32)
        return found

    for copy in copies:
        copy.wait()

    def rows(step, _):
        own = [(step * TALL + row) * 2 + core for row in range(TALL)]
        first, last = own[0] * BLOCK, own[-1] * BLOCK + BLOCK - 1
        low, high = jnp.int32(0), bounds[-1]
        for bound in bounds:
            low = jnp.where(bound <= first, bound, low)
        for bound in reversed(bounds):
            high = jnp.where(bound > last, bound, high)

        def look(column, count):
            listed[count] = column
            taken = pattern[own[0], column]
            for block in own[1:]:
                taken = taken | pattern[block, column]
            return count + taken

        count = lax.fori_loop(low // BLOCK, (high + BLOCK - 1) // BLOCK, look, jnp.int32(0))
        for extra in range(WIDE - 1):
            listed[count + extra] = -1
        steps = (count + WIDE - 1) // WIDE

        tokens = lax.broadcasted_iota(jnp.int32, (BLOCK, BLOCK), 0)
        row_labels = [labels(block * BLOCK + tokens) for block in own]
        lanes = lax.broadcasted_iota(jnp.int32, (1, BLOCK), 1)

        def heads(group, _):
            largest[...] = jnp.full(largest.shape, masked_score, jnp.float32)
            totals[...] = jnp.zeros(totals.shape, jnp.float32)
            combined[...] = jnp.zeros(combined.shape, jnp.float32)

            def columns_of_head(head):
                start = (group * group_heads + head) * HEAD_DIM
                return pl.ds(pl.multiple_of(start, HEAD_DIM), HEAD_DIM)

            def score(chunk, _):
                columns, allowed = [], []
                for part in range(WIDE):
                    entry = listed[chunk * WIDE + part]
                    column = jnp.maximum(entry, 0)
                    columns.append(column)
                    found = jnp.where(entry < 0, -1, labels(column * BLOCK + lanes))
                    allowed.append(
                        jnp.concatenate(
                            [
                                row_labels[row] == jnp.where(pattern[block, column] == 1, found, -1)
                                for row, block in enumerate(own)
                            ],
                            axis=0,
                        )
                    )
                for head in range(group_heads):
                    at = columns_of_head(head)
                    queries = asked[pl.ds(step * TALL, TALL), :, at].reshape(tile, HEAD_DIM)
                    keys = jnp.concatenate([held[column, 0, :, at] for column in columns], axis=0)
                    found = lax.dot_general(
                        queries, keys, (((1,), (1,)), ((), ())), preferred_element_type=jnp.float32
                    )
                    top = largest[head]
                    for part in range(WIDE):
                        span = slice(part * BLOCK, (part + 1) * BLOCK)
                        masked = jnp.where(allowed[part], found[:, span], masked_score)
                        scores[head, chunk, :, span] = masked
                        top = jnp.maximum(top, masked)
                    largest[head] = top
                return 0

            lax.fori_loop(0, steps, score, 0)
            for head in range(group_heads):
                largest[head] = jnp.broadcast_to(
                    jnp.max(largest[head], axis=1, keepdims=True), (tile, BLOCK)
                )

            def combine(chunk, _):
                columns = [jnp.maximum(listed[chunk * WIDE + part], 0) for part in range(WIDE)]
                for head in range(group_heads):
                    at = columns_of_head(head)
                    top, total, weights = largest[head], totals[head], []
                    for part in range(WIDE):
                        span = slice(part * BLOCK, (part + 1) * BLOCK)
                        powers = jnp.exp2((scores[head, chunk, :, span] - top) * exponent_scale)
                        total = total + powers
                        weights.append(powers.astype(jnp.bfloat16))
                    totals[head] = total
                    values = jnp.concatenate([held[column, 1, :, at] for column in columns], axis=0)
                    combined[head] += jnp.dot(
                        jnp.concatenate(weights, axis=1), values, preferred_element_type=jnp.float32
                    )
                return 0

            lax.fori_loop(0, steps, combine, 0)
            for head in range(group_heads):
                total = jnp.sum(totals[head], axis=1, keepdims=True)
                result = (combined[head] / total).astype(jnp.bfloat16)
                out_ref[pl.ds(step * TALL, TALL), :, columns_of_head(head)] = result.reshape(
                    TALL, BLOCK, HEAD_DIM
                )
            return 0

        lax.fori_loop(0, out_ref.shape[2] // (group_heads * HEAD_DIM), heads, 0)
        return 0

    lax.fori_loop(0, 2 * CHIPS // TALL, rows, 0)
    if apart:
        copies = [
            pltpu.make_async_copy(out_ref.at[block_of(slot, core) // 2], out, arrived.at[slot])
            for slot, out in enumerate(outs)
        ]
        for copy in copies:
            copy.start()
        for copy in copies:
            copy.wait()


def attend(pieces, near_other, far_other, position, lengths, pattern, apart):
    places = [where for _, where in pieces]
    pieces = [array for array, _ in pieces]
    kinds, _, width = pieces[0].shape[-3:]
    blocks, tile = 4 * CHIPS, TALL * BLOCK
    heads, count = width // HEAD_DIM, 2 * CHIPS
    per_head = pltpu.VMEM((GROUP, tile, BLOCK), jnp.float32)

    def kernel(*refs):
        attend_kernel(places, apart, *refs)

    return pl.pallas_call(
        kernel,
        out_shape=[jax.ShapeDtypeStruct((BLOCK, width), jnp.bfloat16)] * count
        if apart
        else jax.ShapeDtypeStruct((count, BLOCK, width), jnp.bfloat16),
        in_specs=[IN_SMEM] * 3 + [IN_HBM] * (2 * CHIPS + 2),
        out_specs=[IN_HBM] * count if apart else pl.BlockSpec(memory_space=pltpu.VMEM),
        scratch_shapes=[pltpu.VMEM((count, BLOCK, width), jnp.bfloat16)] * apart
        + [
            pltpu.VMEM((count, BLOCK, width), jnp.bfloat16),
            pltpu.VMEM((blocks, kinds - 1, BLOCK, width), jnp.bfloat16),
            pltpu.VMEM((GROUP, -(-blocks // WIDE), tile, WIDE * BLOCK), jnp.float32),
            per_head,
            per_head,
            per_head,
            pltpu.SMEM((blocks + WIDE,), jnp.int32),
            pltpu.SemaphoreType.DMA((6 * CHIPS,)),
        ],
        compiler_params=pltpu.CompilerParams(vmem_limit_bytes=CUT_VMEM),
        cost_estimate=pl.CostEstimate(
            flops=2 * heads * count * blocks * BLOCK * BLOCK * HEAD_DIM,
            bytes_accessed=2 * blocks * kinds * BLOCK * width,
            transcendentals=heads * count * blocks * BLOCK * BLOCK // 2,
        ),
        name="attend",
    )(lengths, pattern, position, *pieces, near_other, far_other)


def per_device(projected_up, projected_down, lengths_up, lengths_down, pattern_up, pattern_down):
    sections, ranks = lax.axis_size("section"), lax.axis_size("ctx")
    blocks, clips = pattern_down.shape[1], lengths_down.shape[1]
    rank = lax.axis_index("ctx").astype(jnp.int32)
    position = jnp.stack([rank // (2 * CHIPS), (rank // 2) % CHIPS, rank % 2])

    def moved(value, flip, steps=0):
        pairs = [
            (section * ranks + rank, (section + steps) % sections * ranks + (rank ^ flip))
            for section in range(sections)
            for rank in range(ranks)
        ]
        return lax.ppermute(value, ("section", "ctx"), pairs)

    def across(value, steps=0):
        return moved(value, 2 * CHIPS, steps)

    def along(pieces):
        return [moved(piece, 2 * offset) if offset else piece for offset, piece in enumerate(pieces)]

    def after(value, *earlier):
        return lax.optimization_barrier((value, *earlier))[0]

    up = projected_up[0].transpose(1, 0, 2)
    down = projected_down[0].transpose(1, 0, 2)

    piece = (*up.shape[:2], up.shape[2] // (2 * CHIPS))

    chips = [[chip * 2 + core for chip in range(2 * CHIPS)] for core in range(2)]

    def spread(pieces):
        return lax.all_to_all(
            pieces, "ctx", split_axis=0, concat_axis=0, axis_index_groups=chips, tiled=True
        )

    up_far = cut_side(up, position, piece, 1)
    both = cut_both(after(up, up_far), down, position, piece, range(CHIPS))
    down_near = cut_each(after(down, both[0]), position, piece, 0)
    up_far = across(up_far)
    both = along(both)
    up_rest = separate(up_far, position)
    both, up_rest, down_near = lax.optimization_barrier((both, up_rest, down_near))

    up_near, down_far = regroup(both, position)
    down_far = across(down_far)
    up_rest = along([None, *up_rest])[1:]
    up_near_other = moved(up_near, 1)
    up_rest, down_near, up_near_other = lax.optimization_barrier(
        (up_rest, down_near, up_near_other)
    )

    down_near = along(down_near)
    up_far = [(up_far, 0)] + [(array, None) for array in up_rest]
    up_near = [(array, 0) for array in both]
    up_far_other = moved(gather(up_far, position), 1)
    up_out = attend(
        up_near + up_far, up_near_other, up_far_other,
        position, lengths_up[0], pattern_up[0], False,
    )
    down_near, down_far, up_out = lax.optimization_barrier((down_near, down_far, up_out))

    up_out = spread(up_out)
    down_near = [(array, None) for array in down_near]
    down_near_other = moved(gather(down_near, position), 1)
    down_far_other = moved(down_far, 1)
    down_far = [(down_far, index) for index in range(CHIPS)]
    down_out = attend(
        down_near + down_far, down_near_other, down_far_other,
        position, lengths_down[0], pattern_down[0], True,
    )

    up_out, down_out = lax.optimization_barrier((up_out, down_out))
    up_out = moved(up_out, 0, 1)
    down_out = [moved(out, 2 * chip, -1) for chip, out in enumerate(down_out)]
    return join(up_out, position)[None], join(down_out, position)[None]


def solution(mesh):
    in_specs = (
        P("section", "ctx", None, None),
        P("section", "ctx", None, None),
        P("section", None),
        P("section", None),
        P("section", None, None),
        P("section", None, None),
    )
    out_specs = (P("section", "ctx", None), P("section", "ctx", None))
    return jax.shard_map(
        per_device, mesh=mesh, in_specs=in_specs, out_specs=out_specs, check_vma=False
    )
```

```python
import functools
import math

import jax
import jax.numpy as jnp
from jax import lax
from jax.experimental import pallas as pl
from jax.experimental.pallas import tpu as pltpu
from jax.sharding import PartitionSpec as P

HEAD_DIM = 128
BLOCK = 128
TALL = 2
WIDE = 4
GROUP = 6
CHIPS = 4
CUT_VMEM = 60 * 1024 * 1024

masked_score = -1e30
exponent_scale = math.log2(math.e) / math.sqrt(HEAD_DIM)

IN_HBM = pl.BlockSpec(memory_space=pl.ANY)
IN_SMEM = pl.BlockSpec(memory_space=pltpu.SMEM)


def carry(sources, targets, held, arrived, left):
    arrivals, departures = [], []
    for slot, (source, target) in enumerate(zip(sources, targets)):
        arrivals.append(pltpu.make_async_copy(source, held.at[slot], arrived.at[slot]))
        departures.append(pltpu.make_async_copy(held.at[slot], target, left.at[slot]))
    for arrival in arrivals:
        arrival.start()
    for arrival, departure in zip(arrivals, departures):
        arrival.wait()
        departure.start()
    for departure in departures:
        departure.wait()


def carry_scratch(count, shape):
    return [
        pltpu.VMEM((count, *shape), jnp.bfloat16),
        pltpu.SemaphoreType.DMA((count,)),
        pltpu.SemaphoreType.DMA((count,)),
    ]


def columns_of(side, place, offset, width):
    chip = side * CHIPS + (place ^ offset)
    return pl.ds(pl.multiple_of(chip * width, width), width)


def copied(plan, inputs, shapes, position, name, piece=None):
    piece = piece or shapes[0][-3:]
    count = len(plan(None, [None] * len(inputs), [None] * len(shapes), True))

    def kernel(position, *refs):
        ins, outs = refs[: len(inputs)], refs[len(inputs) : len(inputs) + len(shapes)]
        pairs = plan(position, ins, outs, False)
        carry([pair[0] for pair in pairs], [pair[1] for pair in pairs], *refs[-3:])

    return pl.pallas_call(
        kernel,
        out_shape=[jax.ShapeDtypeStruct(shape, jnp.bfloat16) for shape in shapes],
        in_specs=[IN_SMEM] + [IN_HBM] * len(inputs),
        out_specs=[IN_HBM] * len(shapes),
        scratch_shapes=carry_scratch(count, piece),
        compiler_params=pltpu.CompilerParams(vmem_limit_bytes=CUT_VMEM),
        name=name,
    )(position, *inputs)


def cut_from(rows, position, side, offset, width):
    return rows.at[:, :, columns_of(position[0] ^ side, position[1], offset, width)]


def cut_side(rows, position, piece, side):
    def plan(position, ins, outs, dry):
        if dry:
            return range(CHIPS)
        return [
            (cut_from(ins[0], position, side, offset, piece[-1]), outs[0].at[offset])
            for offset in range(CHIPS)
        ]

    return copied(plan, [rows], [(CHIPS, *piece)], position, "cut_side")[0]


def cut_both(up, down, position, piece, offsets):
    def plan(position, ins, outs, dry):
        if dry:
            return range(2 * len(offsets))
        pairs = []
        for out, offset in zip(outs, offsets):
            for part in range(2):
                source = cut_from(ins[part], position, part, offset, piece[-1])
                pairs.append((source, out.at[part]))
        return pairs

    return copied(plan, [up, down], [(2, *piece)] * len(offsets), position, "cut_both")


def cut_each(rows, position, piece, side):
    def plan(position, ins, outs, dry):
        if dry:
            return range(CHIPS)
        return [
            (cut_from(ins[0], position, side, offset, piece[-1]), outs[offset])
            for offset in range(CHIPS)
        ]

    return copied(plan, [rows], [piece] * CHIPS, position, "cut_each")


def regroup(spread, position):
    piece = spread[0].shape[1:]

    def plan(position, ins, outs, dry):
        if dry:
            return range(2 * CHIPS)
        return [
            (ins[index].at[side], outs[side].at[index])
            for side in (1, 0)
            for index in range(CHIPS)
        ]

    return copied(plan, spread, [(CHIPS, *piece)] * 2, position, "regroup")


def separate(pieces, position):
    shape = pieces.shape[1:]

    def plan(position, ins, outs, dry):
        if dry:
            return range(CHIPS - 1)
        return [(ins[0].at[index + 1], outs[index]) for index in range(CHIPS - 1)]

    return copied(plan, [pieces], [shape] * (CHIPS - 1), position, "separate")


def gather(sources, position):
    arrays = [array for array, _ in sources]
    piece = (2, *arrays[0].shape[-2:])

    def plan(position, ins, outs, dry):
        if dry:
            return range(CHIPS)
        return [
            (part(ins[index], where).at[pl.ds(1, 2)], outs[0].at[index])
            for index, (_, where) in enumerate(sources)
        ]

    return copied(plan, arrays, [(CHIPS, *piece)], position, "gather")[0]


def part(ref, where):
    return ref if where is None else ref.at[where]


def join(pieces, position):
    tokens, width = pieces[0].shape
    count = len(pieces)

    def plan(position, ins, outs, dry):
        if dry:
            return range(count)
        if len(ins) == 1:
            return [
                (ins[0].at[chip], outs[0].at[:, pl.ds(chip * width, width)])
                for chip in range(count)
            ]
        pairs = []
        for index, ref in enumerate(ins):
            side, offset = index // CHIPS, index % CHIPS
            columns = columns_of(position[0] ^ side, position[1], offset, width)
            pairs.append((ref, outs[0].at[:, columns]))
        return pairs

    inputs = pieces if isinstance(pieces, list) else [pieces]
    shape = (tokens, count * width)
    return copied(plan, inputs, [shape], position, "join", (tokens, width))[0]


def attend_kernel(places, side, lengths, pattern, position, *refs):
    pieces = refs[: 2 * CHIPS]
    near_other, far_other = refs[2 * CHIPS : 2 * CHIPS + 2]
    apart = side is not None
    scratch = refs[-9:] if apart else refs[-8:]
    asked, held, scores, largest, totals, combined, listed, arrived = scratch[-8:]
    outs = refs[2 * CHIPS + 2 : -len(scratch)]
    out_ref = scratch[0] if apart else outs[0]
    blocks = held.shape[0]
    group_heads = largest.shape[0]
    tile = TALL * BLOCK
    core = position[2]

    def block_of(piece, core):
        return (position[0] ^ (piece // CHIPS)) * (2 * CHIPS) + (
            (position[1] ^ (piece % CHIPS)) * 2 + core
        )

    copies = []
    for piece in range(2 * CHIPS):
        if apart:
            slot = piece % CHIPS
        else:
            slot = block_of(piece, core) // 2
        if side in (None, piece // CHIPS):
            copies.append((part(pieces[piece], places[piece]).at[0], asked.at[slot]))
        mine = part(pieces[piece], places[piece]).at[pl.ds(1, 2)]
        copies.append((mine, held.at[block_of(piece, core)]))
        other = (near_other if piece < CHIPS else far_other).at[piece % CHIPS]
        if other.shape[0] == 3:
            other = other.at[pl.ds(1, 2)]
        copies.append((other, held.at[block_of(piece, 1 - core)]))
    copies = [
        pltpu.make_async_copy(source, target, arrived.at[index])
        for index, (source, target) in enumerate(copies)
    ]
    for copy in copies:
        copy.start()

    bounds = []
    bound = jnp.int32(0)
    for clip in range(lengths.shape[0]):
        bound = bound + lengths[clip]
        bounds.append(bound)

    def labels(tokens):
        found = jnp.zeros(tokens.shape, jnp.int32)
        for bound in bounds:
            found = found + (tokens >= bound).astype(jnp.int32)
        return found

    for copy in copies:
        copy.wait()

    def rows(step, _):
        if apart:
            own = [block_of(side * CHIPS + step * TALL + row, core) for row in range(TALL)]
        else:
            own = [(step * TALL + row) * 2 + core for row in range(TALL)]
        first, last = own[0], own[0]
        for block in own[1:]:
            first, last = jnp.minimum(first, block), jnp.maximum(last, block)
        first, last = first * BLOCK, last * BLOCK + BLOCK - 1
        low, high = jnp.int32(0), bounds[-1]
        for bound in bounds:
            low = jnp.where(bound <= first, bound, low)
        for bound in reversed(bounds):
            high = jnp.where(bound > last, bound, high)

        def look(column, count):
            listed[count] = column
            taken = pattern[own[0], column]
            for block in own[1:]:
                taken = taken | pattern[block, column]
            return count + taken

        count = lax.fori_loop(low // BLOCK, (high + BLOCK - 1) // BLOCK, look, jnp.int32(0))
        for extra in range(WIDE - 1):
            listed[count + extra] = -1
        steps = (count + WIDE - 1) // WIDE

        tokens = lax.broadcasted_iota(jnp.int32, (BLOCK, BLOCK), 0)
        row_labels = [labels(block * BLOCK + tokens) for block in own]
        lanes = lax.broadcasted_iota(jnp.int32, (1, BLOCK), 1)

        def heads(group, _):
            largest[...] = jnp.full(largest.shape, masked_score, jnp.float32)
            totals[...] = jnp.zeros(totals.shape, jnp.float32)
            combined[...] = jnp.zeros(combined.shape, jnp.float32)

            def columns_of_head(head):
                start = (group * group_heads + head) * HEAD_DIM
                return pl.ds(pl.multiple_of(start, HEAD_DIM), HEAD_DIM)

            def score(chunk, _):
                columns, allowed = [], []
                for part in range(WIDE):
                    entry = listed[chunk * WIDE + part]
                    column = jnp.maximum(entry, 0)
                    columns.append(column)
                    found = jnp.where(entry < 0, -1, labels(column * BLOCK + lanes))
                    allowed.append(
                        jnp.concatenate(
                            [
                                row_labels[row] == jnp.where(pattern[block, column] == 1, found, -1)
                                for row, block in enumerate(own)
                            ],
                            axis=0,
                        )
                    )
                for head in range(group_heads):
                    at = columns_of_head(head)
                    queries = asked[pl.ds(step * TALL, TALL), :, at].reshape(tile, HEAD_DIM)
                    keys = jnp.concatenate([held[column, 0, :, at] for column in columns], axis=0)
                    found = lax.dot_general(
                        queries, keys, (((1,), (1,)), ((), ())), preferred_element_type=jnp.float32
                    )
                    top = largest[head]
                    for part in range(WIDE):
                        span = slice(part * BLOCK, (part + 1) * BLOCK)
                        masked = jnp.where(allowed[part], found[:, span], masked_score)
                        scores[head, chunk, :, span] = masked
                        top = jnp.maximum(top, masked)
                    largest[head] = top
                return 0

            lax.fori_loop(0, steps, score, 0)
            for head in range(group_heads):
                largest[head] = jnp.broadcast_to(
                    jnp.max(largest[head], axis=1, keepdims=True), (tile, BLOCK)
                )

            def combine(chunk, _):
                columns = [jnp.maximum(listed[chunk * WIDE + part], 0) for part in range(WIDE)]
                for head in range(group_heads):
                    at = columns_of_head(head)
                    top, total, weights = largest[head], totals[head], []
                    for part in range(WIDE):
                        span = slice(part * BLOCK, (part + 1) * BLOCK)
                        powers = jnp.exp2((scores[head, chunk, :, span] - top) * exponent_scale)
                        total = total + powers
                        weights.append(powers.astype(jnp.bfloat16))
                    totals[head] = total
                    values = jnp.concatenate([held[column, 1, :, at] for column in columns], axis=0)
                    combined[head] += jnp.dot(
                        jnp.concatenate(weights, axis=1), values, preferred_element_type=jnp.float32
                    )
                return 0

            lax.fori_loop(0, steps, combine, 0)
            for head in range(group_heads):
                total = jnp.sum(totals[head], axis=1, keepdims=True)
                result = (combined[head] / total).astype(jnp.bfloat16)
                out_ref[pl.ds(step * TALL, TALL), :, columns_of_head(head)] = result.reshape(
                    TALL, BLOCK, HEAD_DIM
                )
            return 0

        lax.fori_loop(0, out_ref.shape[2] // (group_heads * HEAD_DIM), heads, 0)
        return 0

    lax.fori_loop(0, out_ref.shape[0] // TALL, rows, 0)
    if apart:
        copies = [
            pltpu.make_async_copy(out_ref.at[slot], out, arrived.at[slot])
            for slot, out in enumerate(outs)
        ]
        for copy in copies:
            copy.start()
        for copy in copies:
            copy.wait()


def attend(pieces, near_other, far_other, position, lengths, pattern, side=None):
    places = [where for _, where in pieces]
    pieces = [array for array, _ in pieces]
    kinds, _, width = pieces[0].shape[-3:]
    blocks, tile = 4 * CHIPS, TALL * BLOCK
    heads, apart = width // HEAD_DIM, side is not None
    count = CHIPS if apart else 2 * CHIPS
    per_head = pltpu.VMEM((GROUP, tile, BLOCK), jnp.float32)

    def kernel(*refs):
        attend_kernel(places, side, *refs)

    return pl.pallas_call(
        kernel,
        out_shape=[jax.ShapeDtypeStruct((BLOCK, width), jnp.bfloat16)] * count
        if apart
        else jax.ShapeDtypeStruct((count, BLOCK, width), jnp.bfloat16),
        in_specs=[IN_SMEM] * 3 + [IN_HBM] * (2 * CHIPS + 2),
        out_specs=[IN_HBM] * count if apart else pl.BlockSpec(memory_space=pltpu.VMEM),
        scratch_shapes=[pltpu.VMEM((count, BLOCK, width), jnp.bfloat16)] * apart
        + [
            pltpu.VMEM((count, BLOCK, width), jnp.bfloat16),
            pltpu.VMEM((blocks, kinds - 1, BLOCK, width), jnp.bfloat16),
            pltpu.VMEM((GROUP, -(-blocks // WIDE), tile, WIDE * BLOCK), jnp.float32),
            per_head,
            per_head,
            per_head,
            pltpu.SMEM((blocks + WIDE,), jnp.int32),
            pltpu.SemaphoreType.DMA((6 * CHIPS,)),
        ],
        compiler_params=pltpu.CompilerParams(vmem_limit_bytes=CUT_VMEM),
        cost_estimate=pl.CostEstimate(
            flops=2 * heads * count * blocks * BLOCK * BLOCK * HEAD_DIM,
            bytes_accessed=2 * blocks * kinds * BLOCK * width,
            transcendentals=heads * count * blocks * BLOCK * BLOCK // 2,
        ),
        name="attend",
    )(lengths, pattern, position, *pieces, near_other, far_other)


def per_device(projected_up, projected_down, lengths_up, lengths_down, pattern_up, pattern_down):
    sections, ranks = lax.axis_size("section"), lax.axis_size("ctx")
    rank = lax.axis_index("ctx").astype(jnp.int32)
    position = jnp.stack([rank // (2 * CHIPS), (rank // 2) % CHIPS, rank % 2])

    def moved(value, flip, steps=0):
        pairs = [
            (section * ranks + rank, (section + steps) % sections * ranks + (rank ^ flip))
            for section in range(sections)
            for rank in range(ranks)
        ]
        return lax.ppermute(value, ("section", "ctx"), pairs)

    def across(value, steps=0):
        return moved(value, 2 * CHIPS, steps)

    def along(pieces):
        return [moved(piece, 2 * offset) if offset else piece for offset, piece in enumerate(pieces)]

    def after(value, *earlier):
        return lax.optimization_barrier((value, *earlier))[0]

    up = projected_up[0].transpose(1, 0, 2)
    down = projected_down[0].transpose(1, 0, 2)

    piece = (*up.shape[:2], up.shape[2] // (2 * CHIPS))

    chips = [[chip * 2 + core for chip in range(2 * CHIPS)] for core in range(2)]

    def spread(pieces):
        return lax.all_to_all(
            pieces, "ctx", split_axis=0, concat_axis=0, axis_index_groups=chips, tiled=True
        )

    up_far = cut_side(up, position, piece, 1)
    both = cut_both(after(up, up_far), down, position, piece, range(CHIPS))
    down_near = cut_each(after(down, both[0]), position, piece, 0)
    up_far = across(up_far)
    both = along(both)
    up_rest = separate(up_far, position)
    both, up_rest, down_near = lax.optimization_barrier((both, up_rest, down_near))

    up_near, down_far = regroup(both, position)
    down_far = across(down_far)
    up_rest = along([None, *up_rest])[1:]
    up_near_other = moved(up_near, 1)
    up_rest, down_near, up_near_other = lax.optimization_barrier(
        (up_rest, down_near, up_near_other)
    )

    down_near = along(down_near)
    up_far = [(up_far, 0)] + [(array, None) for array in up_rest]
    up_near = [(array, 0) for array in both]
    up_far_other = moved(gather(up_far, position), 1)
    up_out = attend(
        up_near + up_far, up_near_other, up_far_other,
        position, lengths_up[0], pattern_up[0],
    )
    down_near, down_far, up_out = lax.optimization_barrier((down_near, down_far, up_out))

    up_out = spread(up_out)
    down_near = [(array, None) for array in down_near]
    down_near_other = moved(gather(down_near, position), 1)
    down_far_other = moved(down_far, 1)
    down_far = [(down_far, index) for index in range(CHIPS)]
    args = (down_near + down_far, down_near_other, down_far_other)
    clips = (lengths_down[0], pattern_down[0])

    far_out = attend(*args, position, *clips, 1)
    near_out = attend(*args, after(position, far_out[0]), *clips, 0)
    far_out = [moved(out, 2 * CHIPS + 2 * chip, -1) for chip, out in enumerate(far_out)]
    near_out, far_out, up_out = lax.optimization_barrier((near_out, far_out, up_out))
    up_out = moved(up_out, 0, 1)
    near_out = [moved(out, 2 * chip, -1) for chip, out in enumerate(near_out)]
    return join(up_out, position)[None], join(near_out + far_out, position)[None]


def solution(mesh):
    in_specs = (
        P("section", "ctx", None, None),
        P("section", "ctx", None, None),
        P("section", None),
        P("section", None),
        P("section", None, None),
        P("section", None, None),
    )
    out_specs = (P("section", "ctx", None), P("section", "ctx", None))
    return jax.shard_map(
        per_device, mesh=mesh, in_specs=in_specs, out_specs=out_specs, check_vma=False
    )
```

```python
import functools
import math

import jax
import jax.numpy as jnp
from jax import lax
from jax.experimental import pallas as pl
from jax.experimental.pallas import tpu as pltpu
from jax.sharding import PartitionSpec as P

HEAD_DIM = 128
BLOCK = 128
TALL = 2
WIDE = 4
GROUP = 6
CHIPS = 4
CUT_VMEM = 60 * 1024 * 1024

masked_score = -1e30
exponent_scale = math.log2(math.e) / math.sqrt(HEAD_DIM)

IN_HBM = pl.BlockSpec(memory_space=pl.ANY)
IN_SMEM = pl.BlockSpec(memory_space=pltpu.SMEM)


def carry(sources, targets, held, arrived, left):
    arrivals, departures = [], []
    for slot, (source, target) in enumerate(zip(sources, targets)):
        arrivals.append(pltpu.make_async_copy(source, held.at[slot], arrived.at[slot]))
        departures.append(pltpu.make_async_copy(held.at[slot], target, left.at[slot]))
    for arrival in arrivals:
        arrival.start()
    for arrival, departure in zip(arrivals, departures):
        arrival.wait()
        departure.start()
    for departure in departures:
        departure.wait()


def carry_scratch(count, shape):
    return [
        pltpu.VMEM((count, *shape), jnp.bfloat16),
        pltpu.SemaphoreType.DMA((count,)),
        pltpu.SemaphoreType.DMA((count,)),
    ]


def columns_of(side, place, offset, width):
    chip = side * CHIPS + (place ^ offset)
    return pl.ds(pl.multiple_of(chip * width, width), width)


def copied(plan, inputs, shapes, position, name, piece=None):
    piece = piece or shapes[0][-3:]
    count = len(plan(None, [None] * len(inputs), [None] * len(shapes), True))

    def kernel(position, *refs):
        ins, outs = refs[: len(inputs)], refs[len(inputs) : len(inputs) + len(shapes)]
        pairs = plan(position, ins, outs, False)
        carry([pair[0] for pair in pairs], [pair[1] for pair in pairs], *refs[-3:])

    return pl.pallas_call(
        kernel,
        out_shape=[jax.ShapeDtypeStruct(shape, jnp.bfloat16) for shape in shapes],
        in_specs=[IN_SMEM] + [IN_HBM] * len(inputs),
        out_specs=[IN_HBM] * len(shapes),
        scratch_shapes=carry_scratch(count, piece),
        compiler_params=pltpu.CompilerParams(vmem_limit_bytes=CUT_VMEM),
        name=name,
    )(position, *inputs)


def cut_from(rows, position, side, offset, width):
    return rows.at[:, :, columns_of(position[0] ^ side, position[1], offset, width)]


def cut_side(rows, position, piece, side):
    def plan(position, ins, outs, dry):
        if dry:
            return range(CHIPS)
        return [
            (cut_from(ins[0], position, side, offset, piece[-1]), outs[0].at[offset])
            for offset in range(CHIPS)
        ]

    return copied(plan, [rows], [(CHIPS, *piece)], position, "cut_side")[0]


def cut_both(up, down, position, piece, offsets):
    def plan(position, ins, outs, dry):
        if dry:
            return range(2 * len(offsets))
        pairs = []
        for out, offset in zip(outs, offsets):
            for part in range(2):
                source = cut_from(ins[part], position, part, offset, piece[-1])
                pairs.append((source, out.at[part]))
        return pairs

    return copied(plan, [up, down], [(2, *piece)] * len(offsets), position, "cut_both")


def cut_each(rows, position, piece, side):
    def plan(position, ins, outs, dry):
        if dry:
            return range(CHIPS)
        return [
            (cut_from(ins[0], position, side, offset, piece[-1]), outs[offset])
            for offset in range(CHIPS)
        ]

    return copied(plan, [rows], [piece] * CHIPS, position, "cut_each")


def regroup(spread, position):
    piece = spread[0].shape[1:]

    def plan(position, ins, outs, dry):
        if dry:
            return range(2 * CHIPS)
        return [
            (ins[index].at[side], outs[side].at[index])
            for side in (1, 0)
            for index in range(CHIPS)
        ]

    return copied(plan, spread, [(CHIPS, *piece)] * 2, position, "regroup")


def separate(pieces, position):
    shape = pieces.shape[1:]

    def plan(position, ins, outs, dry):
        if dry:
            return range(CHIPS - 1)
        return [(ins[0].at[index + 1], outs[index]) for index in range(CHIPS - 1)]

    return copied(plan, [pieces], [shape] * (CHIPS - 1), position, "separate")


def gather(sources, position):
    arrays = [array for array, _ in sources]
    piece = (2, *arrays[0].shape[-2:])

    def plan(position, ins, outs, dry):
        if dry:
            return range(CHIPS)
        return [
            (part(ins[index], where).at[pl.ds(1, 2)], outs[0].at[index])
            for index, (_, where) in enumerate(sources)
        ]

    return copied(plan, arrays, [(CHIPS, *piece)], position, "gather")[0]


def part(ref, where):
    return ref if where is None else ref.at[where]


def join(pieces, position):
    tokens, width = pieces[0].shape
    count = len(pieces)

    def plan(position, ins, outs, dry):
        if dry:
            return range(count)
        if len(ins) == 1:
            return [
                (ins[0].at[chip], outs[0].at[:, pl.ds(chip * width, width)])
                for chip in range(count)
            ]
        pairs = []
        for index, ref in enumerate(ins):
            side, offset = index // CHIPS, index % CHIPS
            columns = columns_of(position[0] ^ side, position[1], offset, width)
            pairs.append((ref, outs[0].at[:, columns]))
        return pairs

    inputs = pieces if isinstance(pieces, list) else [pieces]
    shape = (tokens, count * width)
    return copied(plan, inputs, [shape], position, "join", (tokens, width))[0]


def attend_kernel(places, side, lengths, pattern, position, *refs):
    pieces = refs[: 2 * CHIPS]
    near_other, far_other = refs[2 * CHIPS : 2 * CHIPS + 2]
    apart = side is not None
    scratch = refs[-9:] if apart else refs[-8:]
    asked, held, scores, largest, totals, combined, listed, arrived = scratch[-8:]
    outs = refs[2 * CHIPS + 2 : -len(scratch)]
    out_ref = scratch[0] if apart else outs[0]
    blocks = held.shape[0]
    group_heads = largest.shape[0]
    tile = TALL * BLOCK
    core = position[2]

    def block_of(piece, core):
        return (position[0] ^ (piece // CHIPS)) * (2 * CHIPS) + (
            (position[1] ^ (piece % CHIPS)) * 2 + core
        )

    early, late = [], []
    for piece in range(2 * CHIPS):
        if apart:
            slot = piece % CHIPS
        else:
            slot = block_of(piece, core) // 2
        mine = part(pieces[piece], places[piece])
        if side in (None, piece // CHIPS):
            early.append((mine.at[0], asked.at[slot]))
        other = (near_other if piece < CHIPS else far_other).at[piece % CHIPS]
        extra = other.shape[0] - 2
        for kind, copies in ((0, early), (1, late)):
            copies.append((mine.at[1 + kind], held.at[block_of(piece, core), kind]))
            copies.append((other.at[extra + kind], held.at[block_of(piece, 1 - core), kind]))
    copies = [
        pltpu.make_async_copy(source, target, arrived.at[index])
        for index, (source, target) in enumerate(early + late)
    ]
    for copy in copies:
        copy.start()
    early, late = copies[: len(early)], copies[len(early) :]

    bounds = []
    bound = jnp.int32(0)
    for clip in range(lengths.shape[0]):
        bound = bound + lengths[clip]
        bounds.append(bound)

    def labels(tokens):
        found = jnp.zeros(tokens.shape, jnp.int32)
        for bound in bounds:
            found = found + (tokens >= bound).astype(jnp.int32)
        return found

    for copy in early:
        copy.wait()

    def rows(step, _):
        if apart:
            own = [block_of(side * CHIPS + step * TALL + row, core) for row in range(TALL)]
        else:
            own = [(step * TALL + row) * 2 + core for row in range(TALL)]
        first, last = own[0], own[0]
        for block in own[1:]:
            first, last = jnp.minimum(first, block), jnp.maximum(last, block)
        first, last = first * BLOCK, last * BLOCK + BLOCK - 1
        low, high = jnp.int32(0), bounds[-1]
        for bound in bounds:
            low = jnp.where(bound <= first, bound, low)
        for bound in reversed(bounds):
            high = jnp.where(bound > last, bound, high)

        def look(column, count):
            listed[count] = column
            taken = pattern[own[0], column]
            for block in own[1:]:
                taken = taken | pattern[block, column]
            return count + taken

        count = lax.fori_loop(low // BLOCK, (high + BLOCK - 1) // BLOCK, look, jnp.int32(0))
        for extra in range(WIDE - 1):
            listed[count + extra] = -1
        steps = (count + WIDE - 1) // WIDE

        tokens = lax.broadcasted_iota(jnp.int32, (BLOCK, BLOCK), 0)
        row_labels = [labels(block * BLOCK + tokens) for block in own]
        lanes = lax.broadcasted_iota(jnp.int32, (1, BLOCK), 1)

        def heads(group, _):
            largest[...] = jnp.full(largest.shape, masked_score, jnp.float32)
            totals[...] = jnp.zeros(totals.shape, jnp.float32)
            combined[...] = jnp.zeros(combined.shape, jnp.float32)

            def columns_of_head(head):
                start = (group * group_heads + head) * HEAD_DIM
                return pl.ds(pl.multiple_of(start, HEAD_DIM), HEAD_DIM)

            def score(chunk, _):
                columns, allowed = [], []
                for part in range(WIDE):
                    entry = listed[chunk * WIDE + part]
                    column = jnp.maximum(entry, 0)
                    columns.append(column)
                    found = jnp.where(entry < 0, -1, labels(column * BLOCK + lanes))
                    allowed.append(
                        jnp.concatenate(
                            [
                                row_labels[row] == jnp.where(pattern[block, column] == 1, found, -1)
                                for row, block in enumerate(own)
                            ],
                            axis=0,
                        )
                    )
                for head in range(group_heads):
                    at = columns_of_head(head)
                    queries = asked[pl.ds(step * TALL, TALL), :, at].reshape(tile, HEAD_DIM)
                    keys = jnp.concatenate([held[column, 0, :, at] for column in columns], axis=0)
                    found = lax.dot_general(
                        queries, keys, (((1,), (1,)), ((), ())), preferred_element_type=jnp.float32
                    )
                    top = largest[head]
                    for part in range(WIDE):
                        span = slice(part * BLOCK, (part + 1) * BLOCK)
                        masked = jnp.where(allowed[part], found[:, span], masked_score)
                        scores[head, chunk, :, span] = masked
                        top = jnp.maximum(top, masked)
                    largest[head] = top
                return 0

            lax.fori_loop(0, steps, score, 0)
            for head in range(group_heads):
                largest[head] = jnp.broadcast_to(
                    jnp.max(largest[head], axis=1, keepdims=True), (tile, BLOCK)
                )

            @pl.when((step == 0) & (group == 0))
            def _():
                for copy in late:
                    copy.wait()

            def combine(chunk, _):
                columns = [jnp.maximum(listed[chunk * WIDE + part], 0) for part in range(WIDE)]
                for head in range(group_heads):
                    at = columns_of_head(head)
                    top, total, weights = largest[head], totals[head], []
                    for part in range(WIDE):
                        span = slice(part * BLOCK, (part + 1) * BLOCK)
                        powers = jnp.exp2((scores[head, chunk, :, span] - top) * exponent_scale)
                        total = total + powers
                        weights.append(powers.astype(jnp.bfloat16))
                    totals[head] = total
                    values = jnp.concatenate([held[column, 1, :, at] for column in columns], axis=0)
                    combined[head] += jnp.dot(
                        jnp.concatenate(weights, axis=1), values, preferred_element_type=jnp.float32
                    )
                return 0

            lax.fori_loop(0, steps, combine, 0)
            for head in range(group_heads):
                total = jnp.sum(totals[head], axis=1, keepdims=True)
                result = (combined[head] / total).astype(jnp.bfloat16)
                out_ref[pl.ds(step * TALL, TALL), :, columns_of_head(head)] = result.reshape(
                    TALL, BLOCK, HEAD_DIM
                )
            return 0

        lax.fori_loop(0, out_ref.shape[2] // (group_heads * HEAD_DIM), heads, 0)
        return 0

    lax.fori_loop(0, out_ref.shape[0] // TALL, rows, 0)
    if apart:
        copies = [
            pltpu.make_async_copy(out_ref.at[slot], out, arrived.at[slot])
            for slot, out in enumerate(outs)
        ]
        for copy in copies:
            copy.start()
        for copy in copies:
            copy.wait()


def attend(pieces, near_other, far_other, position, lengths, pattern, side=None):
    places = [where for _, where in pieces]
    pieces = [array for array, _ in pieces]
    kinds, _, width = pieces[0].shape[-3:]
    blocks, tile = 4 * CHIPS, TALL * BLOCK
    heads, apart = width // HEAD_DIM, side is not None
    count = CHIPS if apart else 2 * CHIPS
    per_head = pltpu.VMEM((GROUP, tile, BLOCK), jnp.float32)

    def kernel(*refs):
        attend_kernel(places, side, *refs)

    return pl.pallas_call(
        kernel,
        out_shape=[jax.ShapeDtypeStruct((BLOCK, width), jnp.bfloat16)] * count
        if apart
        else jax.ShapeDtypeStruct((count, BLOCK, width), jnp.bfloat16),
        in_specs=[IN_SMEM] * 3 + [IN_HBM] * (2 * CHIPS + 2),
        out_specs=[IN_HBM] * count if apart else pl.BlockSpec(memory_space=pltpu.VMEM),
        scratch_shapes=[pltpu.VMEM((count, BLOCK, width), jnp.bfloat16)] * apart
        + [
            pltpu.VMEM((count, BLOCK, width), jnp.bfloat16),
            pltpu.VMEM((blocks, kinds - 1, BLOCK, width), jnp.bfloat16),
            pltpu.VMEM((GROUP, -(-blocks // WIDE), tile, WIDE * BLOCK), jnp.float32),
            per_head,
            per_head,
            per_head,
            pltpu.SMEM((blocks + WIDE,), jnp.int32),
            pltpu.SemaphoreType.DMA((10 * CHIPS,)),
        ],
        compiler_params=pltpu.CompilerParams(vmem_limit_bytes=CUT_VMEM),
        cost_estimate=pl.CostEstimate(
            flops=2 * heads * count * blocks * BLOCK * BLOCK * HEAD_DIM,
            bytes_accessed=2 * blocks * kinds * BLOCK * width,
            transcendentals=heads * count * blocks * BLOCK * BLOCK // 2,
        ),
        name="attend",
    )(lengths, pattern, position, *pieces, near_other, far_other)


def per_device(projected_up, projected_down, lengths_up, lengths_down, pattern_up, pattern_down):
    sections, ranks = lax.axis_size("section"), lax.axis_size("ctx")
    rank = lax.axis_index("ctx").astype(jnp.int32)
    position = jnp.stack([rank // (2 * CHIPS), (rank // 2) % CHIPS, rank % 2])

    def moved(value, flip, steps=0):
        pairs = [
            (section * ranks + rank, (section + steps) % sections * ranks + (rank ^ flip))
            for section in range(sections)
            for rank in range(ranks)
        ]
        return lax.ppermute(value, ("section", "ctx"), pairs)

    def across(value, steps=0):
        return moved(value, 2 * CHIPS, steps)

    def along(pieces):
        return [moved(piece, 2 * offset) if offset else piece for offset, piece in enumerate(pieces)]

    def after(value, *earlier):
        return lax.optimization_barrier((value, *earlier))[0]

    up = projected_up[0].transpose(1, 0, 2)
    down = projected_down[0].transpose(1, 0, 2)

    piece = (*up.shape[:2], up.shape[2] // (2 * CHIPS))

    chips = [[chip * 2 + core for chip in range(2 * CHIPS)] for core in range(2)]

    def spread(pieces):
        return lax.all_to_all(
            pieces, "ctx", split_axis=0, concat_axis=0, axis_index_groups=chips, tiled=True
        )

    up_far = cut_side(up, position, piece, 1)
    both = cut_both(after(up, up_far), down, position, piece, range(CHIPS))
    down_near = cut_each(after(down, both[0]), position, piece, 0)
    up_far = across(up_far)
    both = along(both)
    up_rest = separate(up_far, position)
    both, up_rest, down_near = lax.optimization_barrier((both, up_rest, down_near))

    up_near, down_far = regroup(both, position)
    down_far = across(down_far)
    up_rest = along([None, *up_rest])[1:]
    up_near_other = moved(up_near, 1)
    up_rest, down_near, up_near_other = lax.optimization_barrier(
        (up_rest, down_near, up_near_other)
    )

    down_near = along(down_near)
    up_far = [(up_far, 0)] + [(array, None) for array in up_rest]
    up_near = [(array, 0) for array in both]
    up_far_other = moved(gather(up_far, position), 1)
    up_out = attend(
        up_near + up_far, up_near_other, up_far_other,
        position, lengths_up[0], pattern_up[0],
    )
    down_near, down_far, up_out = lax.optimization_barrier((down_near, down_far, up_out))

    up_out = spread(up_out)
    down_near = [(array, None) for array in down_near]
    down_near_other = moved(gather(down_near, position), 1)
    down_far_other = moved(down_far, 1)
    down_far = [(down_far, index) for index in range(CHIPS)]
    args = (down_near + down_far, down_near_other, down_far_other)
    clips = (lengths_down[0], pattern_down[0])

    far_out = attend(*args, position, *clips, 1)
    near_out = attend(*args, after(position, far_out[0]), *clips, 0)
    far_out = [moved(out, 2 * CHIPS + 2 * chip, -1) for chip, out in enumerate(far_out)]
    near_out, far_out, up_out = lax.optimization_barrier((near_out, far_out, up_out))
    up_out = moved(up_out, 0, 1)
    near_out = [moved(out, 2 * chip, -1) for chip, out in enumerate(near_out)]
    return join(up_out, position)[None], join(near_out + far_out, position)[None]


def solution(mesh):
    in_specs = (
        P("section", "ctx", None, None),
        P("section", "ctx", None, None),
        P("section", None),
        P("section", None),
        P("section", None, None),
        P("section", None, None),
    )
    out_specs = (P("section", "ctx", None), P("section", "ctx", None))
    return jax.shard_map(
        per_device, mesh=mesh, in_specs=in_specs, out_specs=out_specs, check_vma=False
    )
```
